32 devices in a mesh: group: 2 (over y), cache: 8 (over z, x), tensor: 2 (over core).
Axes of the slice: x: 2, y: 2, z: 4, core: 2. Of those that a mesh axis runs over, the one named last changes fastest.
Arguments:
- tokens: bfloat16 [2048, 8192], P(('group', 'cache'), 'tensor'), parts along dimension 0, may hold values from -6 to 6
- tenant_ids: int32 [2048, 1], P(('group', 'cache')), parts along dimension 0, may hold values from 0 to 7; in each aligned block of 128 rows (0 to 127, 128 to 255, ...) at most 32 rows name the same one
- owner_map: int32 [8], replicated, may hold values from 0 to 7, each once
- adapter_a: bfloat16 [8, 8192, 192], P('cache', 'tensor'), may hold values from -0.0625 to 0.0625
- adapter_bq: bfloat16 [8, 64, 8192], P('cache', None, 'tensor'), may hold values from -0.75 to 0.75
- adapter_bkv: bfloat16 [8, 2, 64, 1024], P('cache', None, None, 'tensor'), may hold values from -0.75 to 0.75
Outputs:
- query_delta: bfloat16 [2048, 8192], P(('group', 'cache'), 'tensor'), parts along dimension 0
- kv_delta: bfloat16 [2, 2048, 1024], P(None, ('group', 'cache'), 'tensor'), parts along dimension 1
The draws below stay inside these ranges and needn't reach their ends.
There are 2 independent parts, one for each index of `group`. The reference program is written for one: setup_inputs(seed, part) draws one part's arguments, and reference() takes and returns one part's arrays. A program takes and returns all parts, laid end to end along the dimension named above; an argument that names none is the same for every part. Nothing has to cross between parts.
Inputs may be any that keep to these rules, and one draw needn't show every extreme that they name: `tenant_ids`: in the rows of one cache index (aligned blocks of 128 rows) no tenant appears more than 32 times, and some tenant appears exactly 32 times. `owner_map`: each cache index holds exactly one tenant's adapter.
All inputs are finite; a program needn't handle non-finite values.
Results may differ from the reference program's by a relative error of at most 0.005.
Values may be sent and summed in bfloat16 or wider, within the bound.
A program may use at most 64 MiB of HBM per device.

```python
import math
import jax
import jax.numpy as jnp
import numpy as np
from jax import lax

D = 8192
KVD = 1024
RANK = 64
TOK_DEV = 128
TOKENS = 1024
TENANTS = 8
CAP = 32
N_CACHE = 8


def block_levels(rng, dims, pieces, least, top_value):
    def one(dim, parts):
        steps = jax.random.uniform(jax.random.fold_in(jax.random.fold_in(rng, 6), dim), (parts,), jnp.float32, least / len(pieces), top_value / len(pieces))
        return jnp.repeat(jnp.exp(steps), dims[dim] // parts).reshape((-1,) + (1,) * (len(dims) - dim - 1))

    factor_of = one(*pieces[0])
    for cut in pieces[1:]:
        factor_of = factor_of * one(*cut)
    return factor_of


def shared_out(own_key, own, number, rows, number_of, top, limit, slope):
    order = jax.random.permutation(own_key, number_of)
    packed, common = load_shares(number_of, rows * top, limit, slope, True), load_shares(number_of, rows * top, limit, slope, False)
    places = jnp.arange(number_of)

    def named(lengths, turn):
        used = int((lengths > 0).sum())
        fixed = max(1, used // 4)
        shifted = fixed + (places - fixed + turn * (used - fixed)) % max(1, number_of - fixed)
        return jnp.zeros((number_of,), jnp.int32).at[order[jnp.where(places < fixed, places, shifted)]].set(jnp.asarray(lengths, jnp.int32))

    lengths = jnp.where(number % 4 == 0, named(packed, number // 4), named(common, number - number // 4 - 1))
    mixed = jax.random.permutation(jax.random.fold_in(own, 3), number_of)
    donor, sink = mixed[0:number_of // 2 * 2:2], mixed[1:number_of // 2 * 2:2]
    slack = jnp.minimum(lengths[donor] - 1, limit - lengths[sink]) // 2
    slack = jnp.where((donor == order[0]) | (sink == order[0]) | (lengths[sink] == 0), 0, jnp.maximum(slack, 0))
    shifted = jax.random.randint(jax.random.fold_in(own, 4), (number_of // 2,), 0, 1 << 20) % (slack + 1)
    lengths = lengths.at[donor].add(-shifted).at[sink].add(shifted)
    items = jnp.searchsorted(jnp.cumsum(lengths), jnp.arange(rows * top), side="right").astype(jnp.int32)
    table = items.reshape(top, rows).T
    table = table[jax.random.permutation(jax.random.fold_in(own, 1), rows)]
    turn = jax.random.randint(jax.random.fold_in(own, 2), (rows, 1), 0, top)
    return jnp.take_along_axis(table, (jnp.arange(top)[None, :] + turn) % top, axis=1)


def load_shares(number_of, total, reach, skew, full):
    portions = [(1 << 20) // math.isqrt(grade ** skew) + 1 for grade in range(1, number_of + 1)]
    largest = reach if full else min(reach, max(-(-total // number_of), total * portions[0] // sum(portions)))
    least = 1 if total - largest >= number_of - 1 else 0
    holding, surplus = [largest] + [least] * (number_of - 1), total - largest - least * (number_of - 1)
    while surplus > 0:
        candidates = [i for i in range(1, number_of) if holding[i] < largest] or [i for i in range(1, number_of) if holding[i] < reach]
        whole, budget = sum([portions[i] for i in candidates]), surplus
        for i in candidates:
            extra = min(reach - holding[i], max(1, budget * portions[i] // whole), surplus)
            holding[i] = holding[i] + extra
            surplus = surplus - extra
    return np.array(holding)


def centred(own_key, shape, scale, most, split=(), kind=jnp.bfloat16):
    loudness = block_levels(own_key, shape, split, -0.22, 0.18) if split else 1.0
    result = jax.random.normal(own_key, shape, jnp.float32) * scale * loudness
    return jnp.minimum(jnp.maximum(result, -most), most).astype(kind)


def setup_inputs(seed: int = 0, part: int = 0) -> dict:
    arg_keys = jax.random.split(jax.random.key(seed), 7)
    own_keys = jax.random.split(jax.random.fold_in(arg_keys[6], part), 7)
    tokens = centred(own_keys[0], (TOKENS, D), 1.0, 6.0, ((0, 8), (1, 2)))
    tenant_ids_keys = jax.random.split(jax.random.fold_in(own_keys[1], 1), TOKENS // TOK_DEV)
    tenant_ids_turns = jax.random.permutation(jax.random.fold_in(own_keys[1], 3), TOKENS // TOK_DEV)
    tenant_ids = jax.vmap(lambda own, number: shared_out(jax.random.fold_in(own_keys[1], 2), own, number, TOK_DEV, TENANTS, 1, CAP, 2))(tenant_ids_keys, tenant_ids_turns).reshape((TOKENS, 1))
    owner_map = jax.random.permutation(arg_keys[2], TENANTS).astype(jnp.int32)
    adapter_a = centred(arg_keys[3], (TENANTS, D, 3 * RANK), D ** -0.5, 0.0625, ((0, 8), (1, 2)))
    adapter_bq = centred(arg_keys[4], (TENANTS, RANK, D), RANK ** -0.5, 0.75, ((0, 8), (2, 2)))
    adapter_bkv = centred(arg_keys[5], (TENANTS, 2, RANK, KVD), RANK ** -0.5, 0.75, ((0, 8), (3, 2)))
    return dict(tokens=tokens, tenant_ids=tenant_ids, owner_map=owner_map, adapter_a=adapter_a, adapter_bq=adapter_bq, adapter_bkv=adapter_bkv)


def reference(tokens, tenant_ids, owner_map, adapter_a, adapter_bq, adapter_bkv):
    tenant_of = tenant_ids[:, 0]
    most = N_CACHE * CAP
    q_init = jnp.zeros(tokens.shape, jnp.bfloat16)
    kv_init = jnp.zeros((2, tokens.shape[0], KVD), jnp.bfloat16)

    def per_tenant(carry, tenant):
        q_out, kv_out = carry
        chosen = jnp.argsort((tenant_of != tenant).astype(jnp.int32), stable=True)[:most].astype(jnp.int32)
        valid = (tenant_of[chosen] == tenant)[:, None]
        holder = owner_map[tenant]
        rows = tokens[chosen]
        low = jnp.dot(rows, adapter_a[holder], preferred_element_type=jnp.float32).astype(jnp.bfloat16)
        query = jnp.dot(low[:, :RANK], adapter_bq[holder], preferred_element_type=jnp.float32).astype(jnp.bfloat16)
        keys = jnp.dot(low[:, RANK:2 * RANK], adapter_bkv[holder, 0], preferred_element_type=jnp.float32).astype(jnp.bfloat16)
        values = jnp.dot(low[:, 2 * RANK:], adapter_bkv[holder, 1], preferred_element_type=jnp.float32).astype(jnp.bfloat16)
        zero = jnp.zeros((), jnp.bfloat16)
        q_out = q_out.at[chosen].add(jnp.where(valid, query, zero))
        kv_out = kv_out.at[0, chosen].add(jnp.where(valid, keys, zero))
        kv_out = kv_out.at[1, chosen].add(jnp.where(valid, values, zero))
        return (q_out, kv_out), None

    (q_out, kv_out), unused = lax.scan(per_tenant, (q_init, kv_init), jnp.arange(TENANTS, dtype=jnp.int32))
    return q_out, kv_out
```

```python
import jax
import jax.numpy as jnp
from jax import lax
from jax.sharding import PartitionSpec as P


def project_low(block, local_a):
    return jnp.dot(block, local_a, preferred_element_type=jnp.float32)


def expand_low(low, query_b, kv_b, rank):
    query = jnp.dot(low[:, :rank], query_b, preferred_element_type=jnp.float32).astype(jnp.bfloat16)
    keys = jnp.dot(low[:, rank : 2 * rank], kv_b[0], preferred_element_type=jnp.float32).astype(
        jnp.bfloat16
    )
    values = jnp.dot(low[:, 2 * rank :], kv_b[1], preferred_element_type=jnp.float32).astype(
        jnp.bfloat16
    )
    return (query, jnp.concatenate([keys, values], axis=1))


GATHER_LIMIT = 8 << 20


def expand_at_holder(low, query_b, kv_b, placing, peers, count):
    slots, rows = placing.shape
    rank, half = query_b.shape
    kv_half = kv_b.shape[2]
    query, keyval = expand_low(low, query_b, kv_b, rank)
    query = query.reshape(peers, count, half)
    keyval = keyval.reshape(peers, count, 2 * kv_half)
    back_q = lax.all_to_all(query, "cache", split_axis=0, concat_axis=0, tiled=True)
    back_kv = lax.all_to_all(keyval, "cache", split_axis=0, concat_axis=0, tiled=True)
    gathering = placing.T
    query_delta = jnp.dot(
        gathering, back_q.reshape(slots, half), preferred_element_type=jnp.float32
    ).astype(jnp.bfloat16)
    keyval = jnp.dot(
        gathering, back_kv.reshape(slots, 2 * kv_half), preferred_element_type=jnp.float32
    ).astype(jnp.bfloat16)
    kv_delta = jnp.stack([keyval[:, :kv_half], keyval[:, kv_half:]], axis=0)
    return (query_delta, kv_delta)


def local(tokens, tenant_ids, owner_map, adapter_a, adapter_bq, adapter_bkv):
    rows, half = tokens.shape
    peers = lax.axis_size("cache")
    capacity = max(2, 2 * rows // peers)
    slots = peers * capacity
    tenants = owner_map.shape[0]
    local_a = adapter_a[0]
    query_b = adapter_bq[0]
    kv_b = adapter_bkv[0]
    rank = query_b.shape[0]
    kv_half = kv_b.shape[2]
    tenant_of = tenant_ids[:, 0]
    match = tenant_of[:, None] == jnp.arange(tenants, dtype=jnp.int32)[None, :]
    holder = jnp.sum(jnp.where(match, owner_map[None, :], 0), axis=1)
    hits = (holder[:, None] == jnp.arange(peers, dtype=jnp.int32)[None, :]).astype(jnp.int32)
    before = jnp.cumsum(hits, axis=0) - hits
    place = holder * capacity + jnp.sum(before * hits, axis=1)
    placing = (place[None, :] == jnp.arange(slots, dtype=jnp.int32)[:, None]).astype(jnp.bfloat16)
    outgoing = jnp.dot(placing, tokens, preferred_element_type=jnp.float32).astype(jnp.bfloat16)
    outgoing = outgoing.reshape(peers, capacity, half)
    block = lax.all_to_all(outgoing, "cache", split_axis=0, concat_axis=0, tiled=True)
    count = block.shape[1]
    flat = block.reshape(peers * count, half)
    low = lax.psum(project_low(flat, local_a), "tensor").astype(jnp.bfloat16)
    if peers * (query_b.size + kv_b.size) * 2 > GATHER_LIMIT:
        return expand_at_holder(low, query_b, kv_b, placing, peers, count)
    everyone_q = lax.all_gather(query_b, "cache", axis=0, tiled=True)
    everyone_kv = lax.all_gather(kv_b, "cache", axis=1, tiled=True)
    back = lax.all_to_all(low.reshape(peers, count, 3 * rank), "cache", split_axis=0, concat_axis=0, tiled=True)
    mine = jnp.dot(
        placing.T, back.reshape(slots, 3 * rank), preferred_element_type=jnp.float32
    ).astype(jnp.bfloat16)
    spread = jnp.arange(peers * rank, dtype=jnp.int32)[None, :] // rank == holder[:, None]

    def expand(j, factors):
        part = jnp.tile(mine[:, j * rank : (j + 1) * rank], (1, peers))
        part = jnp.where(spread, part, jnp.zeros((), jnp.bfloat16))
        return jnp.dot(part, factors, preferred_element_type=jnp.float32).astype(jnp.bfloat16)

    kv_delta = jnp.stack([expand(1, everyone_kv[0]), expand(2, everyone_kv[1])], axis=0)
    return (expand(0, everyone_q), kv_delta)


def solution(mesh):
    in_specs = (
        P(("group", "cache"), "tensor"),
        P(("group", "cache"), None),
        P(),
        P("cache", "tensor", None),
        P("cache", None, "tensor"),
        P("cache", None, None, "tensor"),
    )
    out_specs = (P(("group", "cache"), "tensor"), P(None, ("group", "cache"), "tensor"))
    return jax.shard_map(local, mesh=mesh, in_specs=in_specs, out_specs=out_specs, check_vma=False)
```

```python
import jax
import jax.numpy as jnp
from jax import lax
from jax.experimental import pallas as pl
from jax.experimental.pallas import tpu as pltpu
from jax.sharding import PartitionSpec as P


def project_low(block, local_a):
    return jnp.dot(block, local_a, preferred_element_type=jnp.float32)


def expand_low(low, query_b, kv_b, rank):
    query = jnp.dot(low[:, :rank], query_b, preferred_element_type=jnp.float32).astype(jnp.bfloat16)
    keys = jnp.dot(low[:, rank : 2 * rank], kv_b[0], preferred_element_type=jnp.float32).astype(
        jnp.bfloat16
    )
    values = jnp.dot(low[:, 2 * rank :], kv_b[1], preferred_element_type=jnp.float32).astype(
        jnp.bfloat16
    )
    return (query, jnp.concatenate([keys, values], axis=1))


def local(tokens, tenant_ids, owner_map, adapter_a, adapter_bq, adapter_bkv):
    rows, half = tokens.shape
    peers = lax.axis_size("cache")
    capacity = max(2, 2 * rows // peers)
    slots = peers * capacity
    tenants = owner_map.shape[0]
    local_a = adapter_a[0]
    query_b = adapter_bq[0]
    kv_b = adapter_bkv[0]
    rank = query_b.shape[0]
    kv_half = kv_b.shape[2]
    tenant_of = tenant_ids[:, 0]
    match = tenant_of[:, None] == jnp.arange(tenants, dtype=jnp.int32)[None, :]
    holder = jnp.sum(jnp.where(match, owner_map[None, :], 0), axis=1)
    hits = (holder[:, None] == jnp.arange(peers, dtype=jnp.int32)[None, :]).astype(jnp.int32)
    before = jnp.cumsum(hits, axis=0) - hits
    place = holder * capacity + jnp.sum(before * hits, axis=1)
    placing = (place[None, :] == jnp.arange(slots, dtype=jnp.int32)[:, None]).astype(jnp.bfloat16)
    outgoing = jnp.dot(placing, tokens, preferred_element_type=jnp.float32).astype(jnp.bfloat16)
    outgoing = outgoing.reshape(peers, capacity, half)
    block = lax.all_to_all(outgoing, "cache", split_axis=0, concat_axis=0, tiled=True)
    count = block.shape[1]
    flat = block.reshape(peers * count, half)
    low = lax.psum(project_low(flat, local_a), "tensor").astype(jnp.bfloat16)
    query, keyval = expand_low(low, query_b, kv_b, rank)
    query = query.reshape(peers, count, half)
    keyval = keyval.reshape(peers, count, 2 * kv_half)
    back_q = lax.all_to_all(query, "cache", split_axis=0, concat_axis=0, tiled=True)
    back_kv = lax.all_to_all(keyval, "cache", split_axis=0, concat_axis=0, tiled=True)
    gathering = placing.T
    query_delta = jnp.dot(
        gathering, back_q.reshape(slots, half), preferred_element_type=jnp.float32
    ).astype(jnp.bfloat16)
    keyval = jnp.dot(
        gathering, back_kv.reshape(slots, 2 * kv_half), preferred_element_type=jnp.float32
    ).astype(jnp.bfloat16)
    kv_delta = jnp.stack([keyval[:, :kv_half], keyval[:, kv_half:]], axis=0)
    return (query_delta, kv_delta)


MESH = pl.DeviceIdType.MESH
BF16 = jnp.bfloat16


def fused_kernel(
    tokens, tenant_ids, owner_map, factors_a, factors_q, factors_kv, out_q, out_kv,
    pack, got, held, part, other, low_out, low_back,
    tok_send, tok_recv, up_send, up_recv, down_send, down_recv, x_send, x_recv,
    y_send, y_recv, swap_send, swap_recv, low_send, low_recv,
):
    group, me, core = lax.axis_index("group"), lax.axis_index("cache"), lax.axis_index("tensor")
    peers, capacity, half = pack.shape
    rows = tokens.shape[0]
    slots = peers * capacity
    rank = factors_q.shape[0]
    kv_half = factors_kv.shape[2]
    width = half + 2 * kv_half
    levels = peers // 2
    z, x = me // 2, me % 2

    def remote(src, dst, send, recv, to):
        return pltpu.make_async_remote_copy(
            src_ref=src, dst_ref=dst, send_sem=send, recv_sem=recv, device_id=to, device_id_type=MESH
        )

    def cache_peer(index):
        return (group, index, core)

    across = (1 - group, me, core)
    partner = (group, me, 1 - core)

    barrier = pltpu.get_barrier_semaphore()
    for k in range(1, peers):
        pl.semaphore_signal(barrier, inc=1, device_id=cache_peer((me + k) % peers), device_id_type=MESH)
    pl.semaphore_signal(barrier, inc=1, device_id=across, device_id_type=MESH)
    pl.semaphore_signal(barrier, inc=1, device_id=partner, device_id_type=MESH)

    for h in range(2):
        part_rows = pl.ds(h * rank // 2, rank // 2)
        held[me, h, :, 0:half] = factors_q[part_rows, :]
        held[me, h, :, half : half + kv_half] = factors_kv[0, part_rows, :]
        held[me, h, :, half + kv_half : width] = factors_kv[1, part_rows, :]

    pl.semaphore_wait(barrier, peers + 1)

    def factor(owner, send, recv, to):
        return remote(held.at[owner, group], held.at[owner, group], send, recv, to)

    def up(owner, d):
        return factor(owner, up_send.at[d], up_recv.at[d], cache_peer((me + 2) % peers))

    def down(owner, d):
        return factor(owner, down_send.at[d], down_recv.at[d], cache_peer((me + peers - 2) % peers))

    def sideways(owner):
        return factor(owner, x_send.at[owner // 2], x_recv.at[owner // 2], cache_peer(z * 2 + 1 - x))

    def over(owner):
        return factor(owner, y_send.at[owner], y_recv.at[owner], across)

    def over_in(owner):
        return remote(
            held.at[owner, 1 - group], held.at[owner, 1 - group], y_send.at[owner], y_recv.at[owner], across
        )

    pl.when(z < levels - 1)(lambda: up(me, 1).start())
    pl.when(z > 0)(lambda: down(me, 1).start())
    sideways(me).start()

    tenant = tenant_ids[...]
    holder = jnp.zeros((rows, 1), jnp.int32)
    for i in range(peers):
        holder = jnp.where(tenant == i, owner_map[i], holder)
    hits = (holder == lax.broadcasted_iota(jnp.int32, (rows, peers), 1)).astype(jnp.float32)
    earlier = (
        lax.broadcasted_iota(jnp.int32, (rows, rows), 1) < lax.broadcasted_iota(jnp.int32, (rows, rows), 0)
    ).astype(BF16)
    before = jnp.dot(earlier, hits.astype(BF16), preferred_element_type=jnp.float32)
    place = holder.astype(jnp.float32) * capacity + jnp.sum(before * hits, axis=1, keepdims=True)
    gathering = (
        place == lax.broadcasted_iota(jnp.int32, (rows, slots), 1).astype(jnp.float32)
    ).astype(jnp.float32)
    placing = gathering.T.astype(BF16)
    gathering = gathering.astype(BF16)

    step = min(half, 512)
    for start in range(0, half, step):
        cols = pl.ds(start, step)
        pack[:, :, cols] = (
            jnp.dot(placing, tokens[:, cols], preferred_element_type=jnp.float32)
            .astype(BF16)
            .reshape(peers, capacity, step)
        )

    def token_copy(k):
        to = (me + k) % peers
        return remote(pack.at[to], got.at[me], tok_send.at[k], tok_recv.at[k], cache_peer(to))

    def token_in(k):
        src = (me + peers - k) % peers
        return remote(pack.at[src], got.at[src], tok_send.at[k], tok_recv.at[k], cache_peer(src))

    order = sorted(range(1, peers), key=lambda k: abs(k - levels))
    for k in order:
        token_copy(k).start()
    got[me] = pack[me]

    for d in range(1, levels):
        low_owner, high_owner = me - 2 * d, me + 2 * d

        @pl.when(z >= d)
        def _():
            up(low_owner, d).wait_recv()
            if d < levels - 1:
                pl.when(z < levels - 1)(lambda: up(low_owner, d + 1).start())
            sideways(low_owner).start()
            over(low_owner).start()

        @pl.when(z < levels - d)
        def _():
            down(high_owner, d).wait_recv()
            if d < levels - 1:
                pl.when(z > 0)(lambda: down(high_owner, d + 1).start())
            sideways(high_owner).start()
            over(high_owner).start()

    for j in range(levels):
        owner = ((z + j) % levels) * 2 + 1 - x
        sideways(owner).wait_recv()
        over(owner).start()

    for k in order:
        token_in(k).wait_recv()
    part[...] = lax.dot_general(
        got[...].reshape(slots, half), factors_a[...], (((1,), (1,)), ((), ())),
        preferred_element_type=jnp.float32,
    )
    swap = remote(part, other, swap_send, swap_recv, partner)
    swap.start()
    swap.wait_recv()
    low = (part[...] + other[...]).astype(BF16)
    low_out[...] = low.reshape(peers, capacity, 3 * rank)

    def low_copy(k):
        to = (me + k) % peers
        return remote(low_out.at[to], low_back.at[me], low_send.at[k], low_recv.at[k], cache_peer(to))

    def low_in(k):
        src = (me + peers - k) % peers
        return remote(low_out.at[src], low_back.at[src], low_send.at[k], low_recv.at[k], cache_peer(src))

    for k in order:
        low_copy(k).start()
    low_back[me] = low_out[me]

    for k in range(1, peers):
        over_in((me + k) % peers).wait_recv()
    for k in order:
        low_in(k).wait_recv()

    mine = jnp.dot(
        gathering, low_back[...].reshape(slots, 3 * rank), preferred_element_type=jnp.float32
    ).astype(BF16)
    wide = peers * rank
    own = lax.broadcasted_iota(jnp.int32, (rows, wide), 1) // rank == holder

    def spread(j):
        at = lax.broadcasted_iota(jnp.int32, (3 * rank, wide), 0)
        copies = at == lax.broadcasted_iota(jnp.int32, (3 * rank, wide), 1) % rank + j * rank
        tiled = jnp.dot(mine, copies.astype(jnp.float32).astype(BF16), preferred_element_type=jnp.float32)
        return jnp.where(own, tiled, 0.0).astype(BF16)

    def term(left, cols):
        return jnp.dot(
            left, held[:, :, :, cols].reshape(wide, cols.size), preferred_element_type=jnp.float32
        ).astype(BF16)

    left = spread(0)
    for start in range(0, half, step):
        out_q[:, pl.ds(start, step)] = term(left, pl.ds(start, step))
    for j in range(2):
        out_kv[j] = term(spread(j + 1), pl.ds(half + j * kv_half, kv_half))

    pl.when(z < levels - 1)(lambda: up(me, 1).wait_send())
    pl.when(z > 0)(lambda: down(me, 1).wait_send())
    sideways(me).wait_send()
    for d in range(1, levels):
        low_owner, high_owner = me - 2 * d, me + 2 * d

        @pl.when(z >= d)
        def _():
            if d < levels - 1:
                pl.when(z < levels - 1)(lambda: up(low_owner, d + 1).wait_send())
            sideways(low_owner).wait_send()
            over(low_owner).wait_send()

        @pl.when(z < levels - d)
        def _():
            if d < levels - 1:
                pl.when(z > 0)(lambda: down(high_owner, d + 1).wait_send())
            sideways(high_owner).wait_send()
            over(high_owner).wait_send()

    for j in range(levels):
        over(((z + j) % levels) * 2 + 1 - x).wait_send()
    swap.wait_send()
    for k in order:
        token_copy(k).wait_send()
        low_copy(k).wait_send()


def fused(tokens, tenant_ids, owner_map, adapter_a, adapter_bq, adapter_bkv):
    rows, half = tokens.shape
    peers = lax.axis_size("cache")
    capacity = max(2, 2 * rows // peers)
    rank = adapter_bq.shape[1]
    kv_half = adapter_bkv.shape[3]
    levels = peers // 2
    low = (peers, capacity, 3 * rank)
    pairs = [levels, levels, levels, peers]
    sems = [pltpu.SemaphoreType.DMA((peers,))] * 2
    for number in pairs:
        sems += [pltpu.SemaphoreType.DMA((number,))] * 2
    sems += [pltpu.SemaphoreType.DMA] * 2 + [pltpu.SemaphoreType.DMA((peers,))] * 2
    vmem = pl.BlockSpec(memory_space=pltpu.VMEM)
    flops = 2 * rows * half * (2 * rows + 6 * rank + peers * rank)
    return tuple(
        pl.pallas_call(
            fused_kernel,
            out_shape=(
                jax.ShapeDtypeStruct((rows, half), BF16),
                jax.ShapeDtypeStruct((2, rows, kv_half), BF16),
            ),
            in_specs=[vmem, vmem, pl.BlockSpec(memory_space=pltpu.SMEM), vmem, vmem, vmem],
            out_specs=(vmem, vmem),
            scratch_shapes=[
                pltpu.VMEM((peers, capacity, half), BF16),
                pltpu.VMEM((peers, capacity, half), BF16),
                pltpu.VMEM((peers, 2, rank // 2, half + 2 * kv_half), BF16),
                pltpu.VMEM((peers * capacity, 3 * rank), jnp.float32),
                pltpu.VMEM((peers * capacity, 3 * rank), jnp.float32),
                pltpu.VMEM(low, BF16),
                pltpu.VMEM(low, BF16),
                *sems,
            ],
            compiler_params=pltpu.CompilerParams(
                collective_id=0, has_side_effects=True, vmem_limit_bytes=40 << 20
            ),
            cost_estimate=pl.CostEstimate(flops=flops, bytes_accessed=8 << 20, transcendentals=0),
        )(tokens, tenant_ids, owner_map, jnp.swapaxes(adapter_a[0], 0, 1), adapter_bq[0], adapter_bkv[0])
    )


def solution(mesh):
    in_specs = (
        P(("group", "cache"), "tensor"),
        P(("group", "cache"), None),
        P(),
        P("cache", "tensor", None),
        P("cache", None, "tensor"),
        P("cache", None, None, "tensor"),
    )
    out_specs = (P(("group", "cache"), "tensor"), P(None, ("group", "cache"), "tensor"))
    sizes = (mesh.shape["group"], mesh.shape["cache"], mesh.shape["tensor"])
    body = fused if sizes == (2, 8, 2) else local
    return jax.shard_map(body, mesh=mesh, in_specs=in_specs, out_specs=out_specs, check_vma=False)
```

```python
import jax
import jax.numpy as jnp
from jax import lax
from jax.experimental import pallas as pl
from jax.experimental.pallas import tpu as pltpu
from jax.sharding import PartitionSpec as P


def project_low(block, local_a):
    return jnp.dot(block, local_a, preferred_element_type=jnp.float32)


def expand_low(low, query_b, kv_b, rank):
    query = jnp.dot(low[:, :rank], query_b, preferred_element_type=jnp.float32).astype(jnp.bfloat16)
    keys = jnp.dot(low[:, rank : 2 * rank], kv_b[0], preferred_element_type=jnp.float32).astype(
        jnp.bfloat16
    )
    values = jnp.dot(low[:, 2 * rank :], kv_b[1], preferred_element_type=jnp.float32).astype(
        jnp.bfloat16
    )
    return (query, jnp.concatenate([keys, values], axis=1))


def local(tokens, tenant_ids, owner_map, adapter_a, adapter_bq, adapter_bkv):
    rows, half = tokens.shape
    peers = lax.axis_size("cache")
    capacity = max(2, 2 * rows // peers)
    slots = peers * capacity
    tenants = owner_map.shape[0]
    local_a = adapter_a[0]
    query_b = adapter_bq[0]
    kv_b = adapter_bkv[0]
    rank = query_b.shape[0]
    kv_half = kv_b.shape[2]
    tenant_of = tenant_ids[:, 0]
    match = tenant_of[:, None] == jnp.arange(tenants, dtype=jnp.int32)[None, :]
    holder = jnp.sum(jnp.where(match, owner_map[None, :], 0), axis=1)
    hits = (holder[:, None] == jnp.arange(peers, dtype=jnp.int32)[None, :]).astype(jnp.int32)
    before = jnp.cumsum(hits, axis=0) - hits
    place = holder * capacity + jnp.sum(before * hits, axis=1)
    placing = (place[None, :] == jnp.arange(slots, dtype=jnp.int32)[:, None]).astype(jnp.bfloat16)
    outgoing = jnp.dot(placing, tokens, preferred_element_type=jnp.float32).astype(jnp.bfloat16)
    outgoing = outgoing.reshape(peers, capacity, half)
    block = lax.all_to_all(outgoing, "cache", split_axis=0, concat_axis=0, tiled=True)
    count = block.shape[1]
    flat = block.reshape(peers * count, half)
    low = lax.psum(project_low(flat, local_a), "tensor").astype(jnp.bfloat16)
    query, keyval = expand_low(low, query_b, kv_b, rank)
    query = query.reshape(peers, count, half)
    keyval = keyval.reshape(peers, count, 2 * kv_half)
    back_q = lax.all_to_all(query, "cache", split_axis=0, concat_axis=0, tiled=True)
    back_kv = lax.all_to_all(keyval, "cache", split_axis=0, concat_axis=0, tiled=True)
    gathering = placing.T
    query_delta = jnp.dot(
        gathering, back_q.reshape(slots, half), preferred_element_type=jnp.float32
    ).astype(jnp.bfloat16)
    keyval = jnp.dot(
        gathering, back_kv.reshape(slots, 2 * kv_half), preferred_element_type=jnp.float32
    ).astype(jnp.bfloat16)
    kv_delta = jnp.stack([keyval[:, :kv_half], keyval[:, kv_half:]], axis=0)
    return (query_delta, kv_delta)


MESH = pl.DeviceIdType.MESH
BF16 = jnp.bfloat16


def fused_kernel(
    tokens_at, ids_at, owners_at, factors_at, factors_q, factors_kv, out_q, out_kv,
    tokens, tenant_ids, owner_map, factors_a, fetch_sem, pack, got, held, part, other, low_out, low_back,
    tok_send, tok_recv, up_send, up_recv, down_send, down_recv, x_send, x_recv,
    y_send, y_recv, swap_send, swap_recv, low_send, low_recv,
):
    group, me, core = lax.axis_index("group"), lax.axis_index("cache"), lax.axis_index("tensor")
    peers, capacity, half = pack.shape
    rows = tokens.shape[0]
    slots = peers * capacity
    rank = factors_q.shape[0]
    kv_half = factors_kv.shape[2]
    levels = peers // 2
    z, x = me // 2, me % 2

    def remote(src, dst, send, recv, to):
        return pltpu.make_async_remote_copy(
            src_ref=src, dst_ref=dst, send_sem=send, recv_sem=recv, device_id=to, device_id_type=MESH
        )

    def cache_peer(index):
        return (group, index, core)

    across = (1 - group, me, core)
    partner = (group, me, 1 - core)

    barrier = pltpu.get_barrier_semaphore()
    for k in range(1, peers):
        pl.semaphore_signal(barrier, inc=1, device_id=cache_peer((me + k) % peers), device_id_type=MESH)
    pl.semaphore_signal(barrier, inc=1, device_id=across, device_id_type=MESH)
    pl.semaphore_signal(barrier, inc=1, device_id=partner, device_id_type=MESH)

    fetches = []

    def fetch(src, dst):
        copy = pltpu.make_async_copy(src, dst, fetch_sem.at[len(fetches)])
        fetches.append(copy)
        copy.start()
        return copy

    for h in range(2):
        part_rows = pl.ds(h * rank // 2, rank // 2)
        fetch(factors_q.at[part_rows, :], held.at[me, h, :, pl.ds(0, half)])
        for j in range(2):
            fetch(factors_kv.at[j, part_rows, :], held.at[me, h, :, pl.ds(half + j * kv_half, kv_half)])
    own_factors = list(fetches)
    row_data = [fetch(ids_at, tenant_ids), fetch(owners_at, owner_map), fetch(tokens_at, tokens)]
    late = fetch(factors_at, factors_a)
    for copy in own_factors:
        copy.wait()

    pl.semaphore_wait(barrier, peers + 1)

    def factor(owner, send, recv, to):
        return remote(held.at[owner, group], held.at[owner, group], send, recv, to)

    def up(owner, d):
        return factor(owner, up_send.at[d], up_recv.at[d], cache_peer((me + 2) % peers))

    def down(owner, d):
        return factor(owner, down_send.at[d], down_recv.at[d], cache_peer((me + peers - 2) % peers))

    def sideways(owner):
        return factor(owner, x_send.at[owner // 2], x_recv.at[owner // 2], cache_peer(z * 2 + 1 - x))

    def over(owner):
        return factor(owner, y_send.at[owner], y_recv.at[owner], across)

    def over_in(owner):
        return remote(
            held.at[owner, 1 - group], held.at[owner, 1 - group], y_send.at[owner], y_recv.at[owner], across
        )

    pl.when(z < levels - 1)(lambda: up(me, 1).start())
    pl.when(z > 0)(lambda: down(me, 1).start())
    sideways(me).start()

    for copy in row_data:
        copy.wait()
    tenant = jnp.broadcast_to(tenant_ids[...], (rows, rows)).T[:, 0:1]
    matched = tenant == lax.broadcasted_iota(jnp.int32, (rows, peers), 1)
    holder = jnp.sum(jnp.where(matched, owner_map[...].astype(jnp.float32), 0.0), axis=1, keepdims=True)
    holder = holder.astype(jnp.int32)
    hits = (holder == lax.broadcasted_iota(jnp.int32, (rows, peers), 1)).astype(jnp.float32)
    earlier = (
        lax.broadcasted_iota(jnp.int32, (rows, rows), 1) < lax.broadcasted_iota(jnp.int32, (rows, rows), 0)
    ).astype(BF16)
    before = jnp.dot(earlier, hits.astype(BF16), preferred_element_type=jnp.float32)
    place = holder.astype(jnp.float32) * capacity + jnp.sum(before * hits, axis=1, keepdims=True)
    gathering = (
        place == lax.broadcasted_iota(jnp.int32, (rows, slots), 1).astype(jnp.float32)
    ).astype(jnp.float32)
    placing = gathering.T.astype(BF16)
    gathering = gathering.astype(BF16)

    step = min(half, 512)
    for start in range(0, half, step):
        cols = pl.ds(start, step)
        pack[:, :, cols] = (
            jnp.dot(placing, tokens[:, cols], preferred_element_type=jnp.float32)
            .astype(BF16)
            .reshape(peers, capacity, step)
        )

    def token_copy(k):
        to = (me + k) % peers
        return remote(pack.at[to], got.at[me], tok_send.at[k], tok_recv.at[k], cache_peer(to))

    def token_in(k):
        src = (me + peers - k) % peers
        return remote(pack.at[src], got.at[src], tok_send.at[k], tok_recv.at[k], cache_peer(src))

    order = sorted(range(1, peers), key=lambda k: abs(k - levels))
    got[me] = pack[me]

    for d in range(1, levels):
        low_owner, high_owner = me - 2 * d, me + 2 * d

        @pl.when(z >= d)
        def _():
            up(low_owner, d).wait_recv()
            if d < levels - 1:
                pl.when(z < levels - 1)(lambda: up(low_owner, d + 1).start())
            sideways(low_owner).start()
            over(low_owner).start()

        @pl.when(z < levels - d)
        def _():
            down(high_owner, d).wait_recv()
            if d < levels - 1:
                pl.when(z > 0)(lambda: down(high_owner, d + 1).start())
            sideways(high_owner).start()
            over(high_owner).start()

        if d == 2:
            for k in order:
                token_copy(k).start()

    for j in range(levels):
        owner = ((z + j) % levels) * 2 + 1 - x
        sideways(owner).wait_recv()
        over(owner).start()

    for k in order:
        token_in(k).wait_recv()
    late.wait()
    part[...] = lax.dot_general(
        got[...].reshape(slots, half), factors_a[...], (((1,), (1,)), ((), ())),
        preferred_element_type=jnp.float32,
    )
    swap = remote(part, other, swap_send, swap_recv, partner)
    swap.start()
    swap.wait_recv()
    low = (part[...] + other[...]).astype(BF16)
    low_out[...] = low.reshape(peers, capacity, 3 * rank)

    def low_copy(k):
        to = (me + k) % peers
        return remote(low_out.at[to], low_back.at[me], low_send.at[k], low_recv.at[k], cache_peer(to))

    def low_in(k):
        src = (me + peers - k) % peers
        return remote(low_out.at[src], low_back.at[src], low_send.at[k], low_recv.at[k], cache_peer(src))

    for k in order:
        low_copy(k).start()
    low_back[me] = low_out[me]

    for k in range(1, peers):
        over_in((me + k) % peers).wait_recv()
    for k in order:
        low_in(k).wait_recv()

    mine = jnp.dot(
        gathering, low_back[...].reshape(slots, 3 * rank), preferred_element_type=jnp.float32
    ).astype(BF16)
    wide = peers * rank
    own = lax.broadcasted_iota(jnp.int32, (rows, wide), 1) // rank == holder

    def spread(j):
        at = lax.broadcasted_iota(jnp.int32, (3 * rank, wide), 0)
        copies = at == lax.broadcasted_iota(jnp.int32, (3 * rank, wide), 1) % rank + j * rank
        tiled = jnp.dot(mine, copies.astype(jnp.float32).astype(BF16), preferred_element_type=jnp.float32)
        return jnp.where(own, tiled, 0.0).astype(BF16)

    def term(left, cols):
        return jnp.dot(
            left, held[:, :, :, cols].reshape(wide, cols.size), preferred_element_type=jnp.float32
        ).astype(BF16)

    left = spread(0)
    for start in range(0, half, step):
        out_q[:, pl.ds(start, step)] = term(left, pl.ds(start, step))
    for j in range(2):
        out_kv[j] = term(spread(j + 1), pl.ds(half + j * kv_half, kv_half))

    pl.when(z < levels - 1)(lambda: up(me, 1).wait_send())
    pl.when(z > 0)(lambda: down(me, 1).wait_send())
    sideways(me).wait_send()
    for d in range(1, levels):
        low_owner, high_owner = me - 2 * d, me + 2 * d

        @pl.when(z >= d)
        def _():
            if d < levels - 1:
                pl.when(z < levels - 1)(lambda: up(low_owner, d + 1).wait_send())
            sideways(low_owner).wait_send()
            over(low_owner).wait_send()

        @pl.when(z < levels - d)
        def _():
            if d < levels - 1:
                pl.when(z > 0)(lambda: down(high_owner, d + 1).wait_send())
            sideways(high_owner).wait_send()
            over(high_owner).wait_send()

    for j in range(levels):
        over(((z + j) % levels) * 2 + 1 - x).wait_send()
    swap.wait_send()
    for k in order:
        token_copy(k).wait_send()
        low_copy(k).wait_send()


def fused(tokens, tenant_ids, owner_map, adapter_a, adapter_bq, adapter_bkv):
    rows, half = tokens.shape
    peers = lax.axis_size("cache")
    capacity = max(2, 2 * rows // peers)
    rank = adapter_bq.shape[1]
    kv_half = adapter_bkv.shape[3]
    levels = peers // 2
    low = (peers, capacity, 3 * rank)
    pairs = [levels, levels, levels, peers]
    sems = [pltpu.SemaphoreType.DMA((peers,))] * 2
    for number in pairs:
        sems += [pltpu.SemaphoreType.DMA((number,))] * 2
    sems += [pltpu.SemaphoreType.DMA] * 2 + [pltpu.SemaphoreType.DMA((peers,))] * 2
    vmem = pl.BlockSpec(memory_space=pltpu.VMEM)
    flops = 2 * rows * half * (2 * rows + 6 * rank + peers * rank)
    return tuple(
        pl.pallas_call(
            fused_kernel,
            out_shape=(
                jax.ShapeDtypeStruct((rows, half), BF16),
                jax.ShapeDtypeStruct((2, rows, kv_half), BF16),
            ),
            in_specs=[pl.BlockSpec(memory_space=pltpu.HBM)] * 6,
            out_specs=(vmem, vmem),
            scratch_shapes=[
                pltpu.VMEM((rows, half), BF16),
                pltpu.VMEM((1, rows), jnp.int32),
                pltpu.VMEM((1, peers), jnp.int32),
                pltpu.VMEM((3 * rank, half), BF16),
                pltpu.SemaphoreType.DMA((10,)),
                pltpu.VMEM((peers, capacity, half), BF16),
                pltpu.VMEM((peers, capacity, half), BF16),
                pltpu.VMEM((peers, 2, rank // 2, half + 2 * kv_half), BF16),
                pltpu.VMEM((peers * capacity, 3 * rank), jnp.float32),
                pltpu.VMEM((peers * capacity, 3 * rank), jnp.float32),
                pltpu.VMEM(low, BF16),
                pltpu.VMEM(low, BF16),
                *sems,
            ],
            compiler_params=pltpu.CompilerParams(
                collective_id=0, has_side_effects=True, vmem_limit_bytes=56 << 20
            ),
            cost_estimate=pl.CostEstimate(flops=flops, bytes_accessed=8 << 20, transcendentals=0),
        )(
            tokens,
            tenant_ids.reshape(1, rows),
            owner_map.reshape(1, peers),
            jnp.swapaxes(adapter_a[0], 0, 1),
            adapter_bq[0],
            adapter_bkv[0],
        )
    )


def solution(mesh):
    in_specs = (
        P(("group", "cache"), "tensor"),
        P(("group", "cache"), None),
        P(),
        P("cache", "tensor", None),
        P("cache", None, "tensor"),
        P("cache", None, None, "tensor"),
    )
    out_specs = (P(("group", "cache"), "tensor"), P(None, ("group", "cache"), "tensor"))
    sizes = (mesh.shape["group"], mesh.shape["cache"], mesh.shape["tensor"])
    body = fused if sizes == (2, 8, 2) else local
    return jax.shard_map(body, mesh=mesh, in_specs=in_specs, out_specs=out_specs, check_vma=False)
```

```python
import jax
import jax.numpy as jnp
from jax import lax
from jax.experimental import pallas as pl
from jax.experimental.pallas import tpu as pltpu
from jax.sharding import PartitionSpec as P


def project_low(block, local_a):
    return jnp.dot(block, local_a, preferred_element_type=jnp.float32)


def expand_low(low, query_b, kv_b, rank):
    query = jnp.dot(low[:, :rank], query_b, preferred_element_type=jnp.float32).astype(jnp.bfloat16)
    keys = jnp.dot(low[:, rank : 2 * rank], kv_b[0], preferred_element_type=jnp.float32).astype(
        jnp.bfloat16
    )
    values = jnp.dot(low[:, 2 * rank :], kv_b[1], preferred_element_type=jnp.float32).astype(
        jnp.bfloat16
    )
    return (query, jnp.concatenate([keys, values], axis=1))


def local(tokens, tenant_ids, owner_map, adapter_a, adapter_bq, adapter_bkv):
    rows, half = tokens.shape
    peers = lax.axis_size("cache")
    capacity = max(2, 2 * rows // peers)
    slots = peers * capacity
    tenants = owner_map.shape[0]
    local_a = adapter_a[0]
    query_b = adapter_bq[0]
    kv_b = adapter_bkv[0]
    rank = query_b.shape[0]
    kv_half = kv_b.shape[2]
    tenant_of = tenant_ids[:, 0]
    match = tenant_of[:, None] == jnp.arange(tenants, dtype=jnp.int32)[None, :]
    holder = jnp.sum(jnp.where(match, owner_map[None, :], 0), axis=1)
    hits = (holder[:, None] == jnp.arange(peers, dtype=jnp.int32)[None, :]).astype(jnp.int32)
    before = jnp.cumsum(hits, axis=0) - hits
    place = holder * capacity + jnp.sum(before * hits, axis=1)
    placing = (place[None, :] == jnp.arange(slots, dtype=jnp.int32)[:, None]).astype(jnp.bfloat16)
    outgoing = jnp.dot(placing, tokens, preferred_element_type=jnp.float32).astype(jnp.bfloat16)
    outgoing = outgoing.reshape(peers, capacity, half)
    block = lax.all_to_all(outgoing, "cache", split_axis=0, concat_axis=0, tiled=True)
    count = block.shape[1]
    flat = block.reshape(peers * count, half)
    low = lax.psum(project_low(flat, local_a), "tensor").astype(jnp.bfloat16)
    query, keyval = expand_low(low, query_b, kv_b, rank)
    query = query.reshape(peers, count, half)
    keyval = keyval.reshape(peers, count, 2 * kv_half)
    back_q = lax.all_to_all(query, "cache", split_axis=0, concat_axis=0, tiled=True)
    back_kv = lax.all_to_all(keyval, "cache", split_axis=0, concat_axis=0, tiled=True)
    gathering = placing.T
    query_delta = jnp.dot(
        gathering, back_q.reshape(slots, half), preferred_element_type=jnp.float32
    ).astype(jnp.bfloat16)
    keyval = jnp.dot(
        gathering, back_kv.reshape(slots, 2 * kv_half), preferred_element_type=jnp.float32
    ).astype(jnp.bfloat16)
    kv_delta = jnp.stack([keyval[:, :kv_half], keyval[:, kv_half:]], axis=0)
    return (query_delta, kv_delta)


MESH = pl.DeviceIdType.MESH
SPLIT = 5
BF16 = jnp.bfloat16


def fused_kernel(
    tokens_at, ids_at, owners_at, factors_at, factors_q, factors_kv, out_q, out_kv,
    tokens, tenant_ids, owner_map, factors_a, fetch_sem, pack, got, held, part, other, low_out, low_back,
    tok_send, tok_recv, up_send, up_recv, down_send, down_recv, x_send, x_recv,
    y_send, y_recv, swap_send, swap_recv, low_send, low_recv,
):
    group, me, core = lax.axis_index("group"), lax.axis_index("cache"), lax.axis_index("tensor")
    peers, capacity, half = pack.shape
    rows = tokens.shape[0]
    slots = peers * capacity
    rank = factors_q.shape[0]
    kv_half = factors_kv.shape[2]
    levels = peers // 2
    z, x = me // 2, me % 2

    def remote(src, dst, send, recv, to):
        return pltpu.make_async_remote_copy(
            src_ref=src, dst_ref=dst, send_sem=send, recv_sem=recv, device_id=to, device_id_type=MESH
        )

    def cache_peer(index):
        return (group, index, core)

    across = (1 - group, me, core)
    partner = (group, me, 1 - core)

    barrier = pltpu.get_barrier_semaphore()
    for k in range(1, peers):
        pl.semaphore_signal(barrier, inc=1, device_id=cache_peer((me + k) % peers), device_id_type=MESH)
    pl.semaphore_signal(barrier, inc=1, device_id=across, device_id_type=MESH)
    pl.semaphore_signal(barrier, inc=1, device_id=partner, device_id_type=MESH)

    fetches = []

    def fetch(src, dst):
        copy = pltpu.make_async_copy(src, dst, fetch_sem.at[len(fetches)])
        fetches.append(copy)
        copy.start()
        return copy

    for h in range(2):
        part_rows = pl.ds(h * rank // 2, rank // 2)
        fetch(factors_q.at[part_rows, :], held.at[me, h, :, pl.ds(0, half)])
        for j in range(2):
            fetch(factors_kv.at[j, part_rows, :], held.at[me, h, :, pl.ds(half + j * kv_half, kv_half)])
    own_factors = list(fetches)
    row_data = [fetch(ids_at, tenant_ids), fetch(owners_at, owner_map), fetch(tokens_at, tokens)]
    late = fetch(factors_at, factors_a)
    for copy in own_factors:
        copy.wait()

    pl.semaphore_wait(barrier, peers + 1)

    def factor(owner, send, recv, to):
        return remote(held.at[owner, group], held.at[owner, group], send, recv, to)

    def up(owner, d):
        return factor(owner, up_send.at[d], up_recv.at[d], cache_peer((me + 2) % peers))

    def down(owner, d):
        return factor(owner, down_send.at[d], down_recv.at[d], cache_peer((me + peers - 2) % peers))

    def sideways(owner):
        return factor(owner, x_send.at[owner // 2], x_recv.at[owner // 2], cache_peer(z * 2 + 1 - x))

    def over(owner):
        return factor(owner, y_send.at[owner], y_recv.at[owner], across)

    def over_in(owner):
        return remote(
            held.at[owner, 1 - group], held.at[owner, 1 - group], y_send.at[owner], y_recv.at[owner], across
        )

    pl.when(z < levels - 1)(lambda: up(me, 1).start())
    pl.when(z > 0)(lambda: down(me, 1).start())
    sideways(me).start()

    for copy in row_data:
        copy.wait()
    tenant = jnp.broadcast_to(tenant_ids[...], (rows, rows)).T[:, 0:1]
    matched = tenant == lax.broadcasted_iota(jnp.int32, (rows, peers), 1)
    holder = jnp.sum(jnp.where(matched, owner_map[...].astype(jnp.float32), 0.0), axis=1, keepdims=True)
    holder = holder.astype(jnp.int32)
    hits = (holder == lax.broadcasted_iota(jnp.int32, (rows, peers), 1)).astype(jnp.float32)
    earlier = (
        lax.broadcasted_iota(jnp.int32, (rows, rows), 1) < lax.broadcasted_iota(jnp.int32, (rows, rows), 0)
    ).astype(BF16)
    before = jnp.dot(earlier, hits.astype(BF16), preferred_element_type=jnp.float32)
    place = holder.astype(jnp.float32) * capacity + jnp.sum(before * hits, axis=1, keepdims=True)
    gathering = (
        place == lax.broadcasted_iota(jnp.int32, (rows, slots), 1).astype(jnp.float32)
    ).astype(jnp.float32)
    placing = gathering.T.astype(BF16)
    gathering = gathering.astype(BF16)

    step = min(half, 512)
    for start in range(0, half, step):
        cols = pl.ds(start, step)
        pack[:, :, cols] = (
            jnp.dot(placing, tokens[:, cols], preferred_element_type=jnp.float32)
            .astype(BF16)
            .reshape(peers, capacity, step)
        )

    order = sorted(range(1, peers), key=lambda k: abs(k - levels))
    turn = {k: j + 1 for j, k in enumerate(order)}

    def token_copy(k):
        to = (me + k) % peers
        return remote(pack.at[to], got.at[turn[k]], tok_send.at[k], tok_recv.at[k], cache_peer(to))

    def token_in(k):
        src = (me + peers - k) % peers
        return remote(pack.at[src], got.at[turn[k]], tok_send.at[k], tok_recv.at[k], cache_peer(src))

    got[0] = pack[me]

    for d in range(1, levels):
        low_owner, high_owner = me - 2 * d, me + 2 * d

        @pl.when(z >= d)
        def _():
            up(low_owner, d).wait_recv()
            if d < levels - 1:
                pl.when(z < levels - 1)(lambda: up(low_owner, d + 1).start())
            sideways(low_owner).start()
            over(low_owner).start()

        @pl.when(z < levels - d)
        def _():
            down(high_owner, d).wait_recv()
            if d < levels - 1:
                pl.when(z > 0)(lambda: down(high_owner, d + 1).start())
            sideways(high_owner).start()
            over(high_owner).start()

        if d == 2:
            for k in order:
                token_copy(k).start()

    for j in range(levels):
        owner = ((z + j) % levels) * 2 + 1 - x
        sideways(owner).wait_recv()
        over(owner).start()

    def low_copy(k):
        to = (me + peers - k) % peers
        return remote(low_out.at[turn[k]], low_back.at[me], low_send.at[k], low_recv.at[k], cache_peer(to))

    def low_in(k):
        src = (me + k) % peers
        return remote(low_out.at[turn[k]], low_back.at[src], low_send.at[k], low_recv.at[k], cache_peer(src))

    def swap(stage, first, last):
        band = pl.ds(first * capacity, (last - first) * capacity)
        return remote(part.at[band], other.at[band], swap_send.at[stage], swap_recv.at[stage], partner)

    late.wait()
    stages = ((0, SPLIT), (SPLIT, peers))
    for stage, (first, last) in enumerate(stages):
        arrived = order[max(first, 1) - 1 : last - 1]
        for k in arrived:
            token_in(k).wait_recv()
        band = pl.ds(first * capacity, (last - first) * capacity)
        part[band, :] = lax.dot_general(
            got[first:last].reshape((last - first) * capacity, half), factors_a[...],
            (((1,), (1,)), ((), ())), preferred_element_type=jnp.float32,
        )
        swap(stage, first, last).start()
        swap(stage, first, last).wait_recv()
        low = (part[band, :] + other[band, :]).astype(BF16)
        low_out[first:last] = low.reshape(last - first, capacity, 3 * rank)
        for k in arrived:
            low_copy(k).start()
    low_back[me] = low_out[0]

    for k in range(1, peers):
        over_in((me + k) % peers).wait_recv()
    for k in order:
        low_in(k).wait_recv()

    mine = jnp.dot(
        gathering, low_back[...].reshape(slots, 3 * rank), preferred_element_type=jnp.float32
    ).astype(BF16)
    wide = peers * rank
    own = lax.broadcasted_iota(jnp.int32, (rows, wide), 1) // rank == holder

    def spread(j):
        at = lax.broadcasted_iota(jnp.int32, (3 * rank, wide), 0)
        copies = at == lax.broadcasted_iota(jnp.int32, (3 * rank, wide), 1) % rank + j * rank
        tiled = jnp.dot(mine, copies.astype(jnp.float32).astype(BF16), preferred_element_type=jnp.float32)
        return jnp.where(own, tiled, 0.0).astype(BF16)

    def term(left, cols):
        return jnp.dot(
            left, held[:, :, :, cols].reshape(wide, cols.size), preferred_element_type=jnp.float32
        ).astype(BF16)

    left = spread(0)
    for start in range(0, half, step):
        out_q[:, pl.ds(start, step)] = term(left, pl.ds(start, step))
    for j in range(2):
        out_kv[j] = term(spread(j + 1), pl.ds(half + j * kv_half, kv_half))

    pl.when(z < levels - 1)(lambda: up(me, 1).wait_send())
    pl.when(z > 0)(lambda: down(me, 1).wait_send())
    sideways(me).wait_send()
    for d in range(1, levels):
        low_owner, high_owner = me - 2 * d, me + 2 * d

        @pl.when(z >= d)
        def _():
            if d < levels - 1:
                pl.when(z < levels - 1)(lambda: up(low_owner, d + 1).wait_send())
            sideways(low_owner).wait_send()
            over(low_owner).wait_send()

        @pl.when(z < levels - d)
        def _():
            if d < levels - 1:
                pl.when(z > 0)(lambda: down(high_owner, d + 1).wait_send())
            sideways(high_owner).wait_send()
            over(high_owner).wait_send()

    for j in range(levels):
        over(((z + j) % levels) * 2 + 1 - x).wait_send()
    for stage, (first, last) in enumerate(stages):
        swap(stage, first, last).wait_send()
    for k in order:
        token_copy(k).wait_send()
        low_copy(k).wait_send()


def fused(tokens, tenant_ids, owner_map, adapter_a, adapter_bq, adapter_bkv):
    rows, half = tokens.shape
    peers = lax.axis_size("cache")
    capacity = max(2, 2 * rows // peers)
    rank = adapter_bq.shape[1]
    kv_half = adapter_bkv.shape[3]
    levels = peers // 2
    low = (peers, capacity, 3 * rank)
    pairs = [levels, levels, levels, peers]
    sems = [pltpu.SemaphoreType.DMA((peers,))] * 2
    for number in pairs:
        sems += [pltpu.SemaphoreType.DMA((number,))] * 2
    sems += [pltpu.SemaphoreType.DMA((2,))] * 2 + [pltpu.SemaphoreType.DMA((peers,))] * 2
    vmem = pl.BlockSpec(memory_space=pltpu.VMEM)
    flops = 2 * rows * half * (2 * rows + 6 * rank + peers * rank)
    return tuple(
        pl.pallas_call(
            fused_kernel,
            out_shape=(
                pltpu.VMEM((rows, half), BF16),
                pltpu.VMEM((2, rows, kv_half), BF16),
            ),
            in_specs=[pl.BlockSpec(memory_space=pltpu.HBM)] * 6,
            out_specs=(vmem, vmem),
            scratch_shapes=[
                pltpu.VMEM((rows, half), BF16),
                pltpu.VMEM((1, rows), jnp.int32),
                pltpu.VMEM((1, peers), jnp.int32),
                pltpu.VMEM((3 * rank, half), BF16),
                pltpu.SemaphoreType.DMA((10,)),
                pltpu.VMEM((peers, capacity, half), BF16),
                pltpu.VMEM((peers, capacity, half), BF16),
                pltpu.VMEM((peers, 2, rank // 2, half + 2 * kv_half), BF16),
                pltpu.VMEM((peers * capacity, 3 * rank), jnp.float32),
                pltpu.VMEM((peers * capacity, 3 * rank), jnp.float32),
                pltpu.VMEM(low, BF16),
                pltpu.VMEM(low, BF16),
                *sems,
            ],
            compiler_params=pltpu.CompilerParams(
                collective_id=0, has_side_effects=True, vmem_limit_bytes=56 << 20
            ),
            cost_estimate=pl.CostEstimate(flops=flops, bytes_accessed=8 << 20, transcendentals=0),
        )(
            tokens,
            tenant_ids.reshape(1, rows),
            owner_map.reshape(1, peers),
            jnp.swapaxes(adapter_a[0], 0, 1),
            adapter_bq[0],
            adapter_bkv[0],
        )
    )


def solution(mesh):
    in_specs = (
        P(("group", "cache"), "tensor"),
        P(("group", "cache"), None),
        P(),
        P("cache", "tensor", None),
        P("cache", None, "tensor"),
        P("cache", None, None, "tensor"),
    )
    out_specs = (P(("group", "cache"), "tensor"), P(None, ("group", "cache"), "tensor"))
    sizes = (mesh.shape["group"], mesh.shape["cache"], mesh.shape["tensor"])
    body = fused if sizes == (2, 8, 2) else local
    return jax.shard_map(body, mesh=mesh, in_specs=in_specs, out_specs=out_specs, check_vma=False)
```

```python
import jax
import jax.numpy as jnp
from jax import lax
from jax.experimental import pallas as pl
from jax.experimental.pallas import tpu as pltpu
from jax.sharding import PartitionSpec as P


def project_low(block, local_a):
    return jnp.dot(block, local_a, preferred_element_type=jnp.float32)


def expand_low(low, query_b, kv_b, rank):
    query = jnp.dot(low[:, :rank], query_b, preferred_element_type=jnp.float32).astype(jnp.bfloat16)
    keys = jnp.dot(low[:, rank : 2 * rank], kv_b[0], preferred_element_type=jnp.float32).astype(
        jnp.bfloat16
    )
    values = jnp.dot(low[:, 2 * rank :], kv_b[1], preferred_element_type=jnp.float32).astype(
        jnp.bfloat16
    )
    return (query, jnp.concatenate([keys, values], axis=1))


def local(tokens, tenant_ids, owner_map, adapter_a, adapter_bq, adapter_bkv):
    rows, half = tokens.shape
    peers = lax.axis_size("cache")
    capacity = max(2, 2 * rows // peers)
    slots = peers * capacity
    tenants = owner_map.shape[0]
    local_a = adapter_a[0]
    query_b = adapter_bq[0]
    kv_b = adapter_bkv[0]
    rank = query_b.shape[0]
    kv_half = kv_b.shape[2]
    tenant_of = tenant_ids[:, 0]
    match = tenant_of[:, None] == jnp.arange(tenants, dtype=jnp.int32)[None, :]
    holder = jnp.sum(jnp.where(match, owner_map[None, :], 0), axis=1)
    hits = (holder[:, None] == jnp.arange(peers, dtype=jnp.int32)[None, :]).astype(jnp.int32)
    before = jnp.cumsum(hits, axis=0) - hits
    place = holder * capacity + jnp.sum(before * hits, axis=1)
    placing = (place[None, :] == jnp.arange(slots, dtype=jnp.int32)[:, None]).astype(jnp.bfloat16)
    outgoing = jnp.dot(placing, tokens, preferred_element_type=jnp.float32).astype(jnp.bfloat16)
    outgoing = outgoing.reshape(peers, capacity, half)
    block = lax.all_to_all(outgoing, "cache", split_axis=0, concat_axis=0, tiled=True)
    count = block.shape[1]
    flat = block.reshape(peers * count, half)
    low = lax.psum(project_low(flat, local_a), "tensor").astype(jnp.bfloat16)
    query, keyval = expand_low(low, query_b, kv_b, rank)
    query = query.reshape(peers, count, half)
    keyval = keyval.reshape(peers, count, 2 * kv_half)
    back_q = lax.all_to_all(query, "cache", split_axis=0, concat_axis=0, tiled=True)
    back_kv = lax.all_to_all(keyval, "cache", split_axis=0, concat_axis=0, tiled=True)
    gathering = placing.T
    query_delta = jnp.dot(
        gathering, back_q.reshape(slots, half), preferred_element_type=jnp.float32
    ).astype(jnp.bfloat16)
    keyval = jnp.dot(
        gathering, back_kv.reshape(slots, 2 * kv_half), preferred_element_type=jnp.float32
    ).astype(jnp.bfloat16)
    kv_delta = jnp.stack([keyval[:, :kv_half], keyval[:, kv_half:]], axis=0)
    return (query_delta, kv_delta)


MESH = pl.DeviceIdType.MESH
SPLIT = 5
BF16 = jnp.bfloat16


def fused_kernel(
    tokens_at, ids_at, owners_at, factors_at, factors_q, factors_kv, out_q, out_kv,
    tokens, tenant_ids, owner_map, factors_a, fetch_sem, copies, own, pack, got, held, part, other, low_out, low_back,
    tok_send, tok_recv, up_send, up_recv, down_send, down_recv, x_send, x_recv,
    y_send, y_recv, swap_send, swap_recv, low_send, low_recv,
):
    group, me, core = lax.axis_index("group"), lax.axis_index("cache"), lax.axis_index("tensor")
    peers, capacity, half = pack.shape
    rows = tokens.shape[0]
    slots = peers * capacity
    rank = factors_q.shape[0]
    kv_half = factors_kv.shape[2]
    levels = peers // 2
    z, x = me // 2, me % 2

    def remote(src, dst, send, recv, to):
        return pltpu.make_async_remote_copy(
            src_ref=src, dst_ref=dst, send_sem=send, recv_sem=recv, device_id=to, device_id_type=MESH
        )

    def cache_peer(index):
        return (group, index, core)

    across = (1 - group, me, core)
    partner = (group, me, 1 - core)

    barrier = pltpu.get_barrier_semaphore()
    for k in range(1, peers):
        pl.semaphore_signal(barrier, inc=1, device_id=cache_peer((me + k) % peers), device_id_type=MESH)
    pl.semaphore_signal(barrier, inc=1, device_id=across, device_id_type=MESH)
    pl.semaphore_signal(barrier, inc=1, device_id=partner, device_id_type=MESH)

    fetches = []

    def fetch(src, dst):
        copy = pltpu.make_async_copy(src, dst, fetch_sem.at[len(fetches)])
        fetches.append(copy)
        copy.start()
        return copy

    for h in range(2):
        part_rows = pl.ds(h * rank // 2, rank // 2)
        fetch(factors_q.at[part_rows, :], held.at[me, h, :, pl.ds(0, half)])
        for j in range(2):
            fetch(factors_kv.at[j, part_rows, :], held.at[me, h, :, pl.ds(half + j * kv_half, kv_half)])
    own_factors = list(fetches)
    row_data = [fetch(ids_at, tenant_ids), fetch(owners_at, owner_map), fetch(tokens_at, tokens)]
    late = fetch(factors_at, factors_a)
    for copy in own_factors:
        copy.wait()

    pl.semaphore_wait(barrier, peers + 1)

    def factor(owner, send, recv, to):
        return remote(held.at[owner, group], held.at[owner, group], send, recv, to)

    def up(owner, d):
        return factor(owner, up_send.at[d], up_recv.at[d], cache_peer((me + 2) % peers))

    def down(owner, d):
        return factor(owner, down_send.at[d], down_recv.at[d], cache_peer((me + peers - 2) % peers))

    def sideways(owner):
        return factor(owner, x_send.at[owner // 2], x_recv.at[owner // 2], cache_peer(z * 2 + 1 - x))

    def over(owner):
        return factor(owner, y_send.at[owner], y_recv.at[owner], across)

    def over_in(owner):
        return remote(
            held.at[owner, 1 - group], held.at[owner, 1 - group], y_send.at[owner], y_recv.at[owner], across
        )

    pl.when(z < levels - 1)(lambda: up(me, 1).start())
    pl.when(z > 0)(lambda: down(me, 1).start())
    sideways(me).start()

    for copy in row_data:
        copy.wait()
    tenant = jnp.broadcast_to(tenant_ids[...], (rows, rows)).T[:, 0:1]
    matched = tenant == lax.broadcasted_iota(jnp.int32, (rows, peers), 1)
    holder = jnp.sum(jnp.where(matched, owner_map[...].astype(jnp.float32), 0.0), axis=1, keepdims=True)
    holder = holder.astype(jnp.int32)
    hits = (holder == lax.broadcasted_iota(jnp.int32, (rows, peers), 1)).astype(jnp.float32)
    earlier = (
        lax.broadcasted_iota(jnp.int32, (rows, rows), 1) < lax.broadcasted_iota(jnp.int32, (rows, rows), 0)
    ).astype(BF16)
    before = jnp.dot(earlier, hits.astype(BF16), preferred_element_type=jnp.float32)
    place = holder.astype(jnp.float32) * capacity + jnp.sum(before * hits, axis=1, keepdims=True)
    gathering = (
        place == lax.broadcasted_iota(jnp.int32, (rows, slots), 1).astype(jnp.float32)
    ).astype(jnp.float32)
    placing = gathering.T.astype(BF16)
    gathering = gathering.astype(BF16)

    step = min(half, 512)
    for start in range(0, half, step):
        cols = pl.ds(start, step)
        pack[:, :, cols] = (
            jnp.dot(placing, tokens[:, cols], preferred_element_type=jnp.float32)
            .astype(BF16)
            .reshape(peers, capacity, step)
        )

    order = sorted(range(1, peers), key=lambda k: abs(k - levels))
    turn = {k: j + 1 for j, k in enumerate(order)}

    def token_copy(k):
        to = (me + k) % peers
        return remote(pack.at[to], got.at[turn[k]], tok_send.at[k], tok_recv.at[k], cache_peer(to))

    def token_in(k):
        src = (me + peers - k) % peers
        return remote(pack.at[src], got.at[turn[k]], tok_send.at[k], tok_recv.at[k], cache_peer(src))

    got[0] = pack[me]
    wide = peers * rank
    own[...] = (lax.broadcasted_iota(jnp.int32, (rows, wide), 1) // rank == holder).astype(jnp.float32)
    for j in range(3):
        same = (
            lax.broadcasted_iota(jnp.int32, (3 * rank, wide), 0)
            == lax.broadcasted_iota(jnp.int32, (3 * rank, wide), 1) % rank + j * rank
        )
        copies[j] = same.astype(jnp.float32).astype(BF16)

    for d in range(1, levels):
        low_owner, high_owner = me - 2 * d, me + 2 * d

        @pl.when(z >= d)
        def _():
            up(low_owner, d).wait_recv()
            if d < levels - 1:
                pl.when(z < levels - 1)(lambda: up(low_owner, d + 1).start())
            sideways(low_owner).start()
            over(low_owner).start()

        @pl.when(z < levels - d)
        def _():
            down(high_owner, d).wait_recv()
            if d < levels - 1:
                pl.when(z > 0)(lambda: down(high_owner, d + 1).start())
            sideways(high_owner).start()
            over(high_owner).start()

        if d == 2:
            for k in order:
                token_copy(k).start()

    for j in range(levels):
        owner = ((z + j) % levels) * 2 + 1 - x
        sideways(owner).wait_recv()
        over(owner).start()

    def low_copy(k):
        to = (me + peers - k) % peers
        return remote(low_out.at[turn[k]], low_back.at[me], low_send.at[k], low_recv.at[k], cache_peer(to))

    def low_in(k):
        src = (me + k) % peers
        return remote(low_out.at[turn[k]], low_back.at[src], low_send.at[k], low_recv.at[k], cache_peer(src))

    def swap(stage, first, last):
        band = pl.ds(first * capacity, (last - first) * capacity)
        return remote(part.at[band], other.at[band], swap_send.at[stage], swap_recv.at[stage], partner)

    late.wait()
    stages = ((0, SPLIT), (SPLIT, peers))
    for stage, (first, last) in enumerate(stages):
        arrived = order[max(first, 1) - 1 : last - 1]
        for k in arrived:
            token_in(k).wait_recv()
        band = pl.ds(first * capacity, (last - first) * capacity)
        part[band, :] = lax.dot_general(
            got[first:last].reshape((last - first) * capacity, half), factors_a[...],
            (((1,), (1,)), ((), ())), preferred_element_type=jnp.float32,
        )
        swap(stage, first, last).start()
        swap(stage, first, last).wait_recv()
        low = (part[band, :] + other[band, :]).astype(BF16)
        low_out[first:last] = low.reshape(last - first, capacity, 3 * rank)
        for k in arrived:
            low_copy(k).start()
    low_back[me] = low_out[0]

    for k in range(1, peers):
        over_in((me + k) % peers).wait_recv()
    for k in order:
        low_in(k).wait_recv()

    mine = jnp.dot(
        gathering, low_back[...].reshape(slots, 3 * rank), preferred_element_type=jnp.float32
    ).astype(BF16)
    def spread(j):
        tiled = jnp.dot(mine, copies[j], preferred_element_type=jnp.float32)
        return jnp.where(own[...] > 0.0, tiled, 0.0).astype(BF16)

    def term(left, cols):
        return jnp.dot(
            left, held[:, :, :, cols].reshape(wide, cols.size), preferred_element_type=jnp.float32
        ).astype(BF16)

    left = spread(0)
    for start in range(0, half, step):
        out_q[:, pl.ds(start, step)] = term(left, pl.ds(start, step))
    for j in range(2):
        out_kv[j] = term(spread(j + 1), pl.ds(half + j * kv_half, kv_half))

    pl.when(z < levels - 1)(lambda: up(me, 1).wait_send())
    pl.when(z > 0)(lambda: down(me, 1).wait_send())
    sideways(me).wait_send()
    for d in range(1, levels):
        low_owner, high_owner = me - 2 * d, me + 2 * d

        @pl.when(z >= d)
        def _():
            if d < levels - 1:
                pl.when(z < levels - 1)(lambda: up(low_owner, d + 1).wait_send())
            sideways(low_owner).wait_send()
            over(low_owner).wait_send()

        @pl.when(z < levels - d)
        def _():
            if d < levels - 1:
                pl.when(z > 0)(lambda: down(high_owner, d + 1).wait_send())
            sideways(high_owner).wait_send()
            over(high_owner).wait_send()

    for j in range(levels):
        over(((z + j) % levels) * 2 + 1 - x).wait_send()
    for stage, (first, last) in enumerate(stages):
        swap(stage, first, last).wait_send()
    for k in order:
        token_copy(k).wait_send()
        low_copy(k).wait_send()


def fused(tokens, tenant_ids, owner_map, adapter_a, adapter_bq, adapter_bkv):
    rows, half = tokens.shape
    peers = lax.axis_size("cache")
    capacity = max(2, 2 * rows // peers)
    rank = adapter_bq.shape[1]
    kv_half = adapter_bkv.shape[3]
    levels = peers // 2
    low = (peers, capacity, 3 * rank)
    pairs = [levels, levels, levels, peers]
    sems = [pltpu.SemaphoreType.DMA((peers,))] * 2
    for number in pairs:
        sems += [pltpu.SemaphoreType.DMA((number,))] * 2
    sems += [pltpu.SemaphoreType.DMA((2,))] * 2 + [pltpu.SemaphoreType.DMA((peers,))] * 2
    vmem = pl.BlockSpec(memory_space=pltpu.VMEM)
    flops = 2 * rows * half * (2 * rows + 6 * rank + peers * rank)
    return tuple(
        pl.pallas_call(
            fused_kernel,
            out_shape=(
                pltpu.VMEM((rows, half), BF16),
                pltpu.VMEM((2, rows, kv_half), BF16),
            ),
            in_specs=[pl.BlockSpec(memory_space=pltpu.HBM)] * 6,
            out_specs=(vmem, vmem),
            scratch_shapes=[
                pltpu.VMEM((rows, half), BF16),
                pltpu.VMEM((1, rows), jnp.int32),
                pltpu.VMEM((1, peers), jnp.int32),
                pltpu.VMEM((3 * rank, half), BF16),
                pltpu.SemaphoreType.DMA((10,)),
                pltpu.VMEM((3, 3 * rank, peers * rank), BF16),
                pltpu.VMEM((rows, peers * rank), jnp.float32),
                pltpu.VMEM((peers, capacity, half), BF16),
                pltpu.VMEM((peers, capacity, half), BF16),
                pltpu.VMEM((peers, 2, rank // 2, half + 2 * kv_half), BF16),
                pltpu.VMEM((peers * capacity, 3 * rank), jnp.float32),
                pltpu.VMEM((peers * capacity, 3 * rank), jnp.float32),
                pltpu.VMEM(low, BF16),
                pltpu.VMEM(low, BF16),
                *sems,
            ],
            compiler_params=pltpu.CompilerParams(
                collective_id=0, has_side_effects=True, vmem_limit_bytes=56 << 20
            ),
            cost_estimate=pl.CostEstimate(flops=flops, bytes_accessed=8 << 20, transcendentals=0),
        )(
            tokens,
            tenant_ids.reshape(1, rows),
            owner_map.reshape(1, peers),
            jnp.swapaxes(adapter_a[0], 0, 1),
            adapter_bq[0],
            adapter_bkv[0],
        )
    )


def solution(mesh):
    in_specs = (
        P(("group", "cache"), "tensor"),
        P(("group", "cache"), None),
        P(),
        P("cache", "tensor", None),
        P("cache", None, "tensor"),
        P("cache", None, None, "tensor"),
    )
    out_specs = (P(("group", "cache"), "tensor"), P(None, ("group", "cache"), "tensor"))
    sizes = (mesh.shape["group"], mesh.shape["cache"], mesh.shape["tensor"])
    body = fused if sizes == (2, 8, 2) else local
    return jax.shard_map(body, mesh=mesh, in_specs=in_specs, out_specs=out_specs, check_vma=False)
```
